512 devices in a mesh: dp: 8 (over z), fsdp: 64 (over x, y, core).
Axes of the slice: x: 4, y: 8, z: 8, core: 2. Of those that a mesh axis runs over, the one named last changes fastest.
Arguments:
- grad_parts: bfloat16 [8, 224, 512, 512], P('dp', None, 'fsdp'), may hold values from -4 to 4
- owner_map: int32 [224], replicated, may hold values from 0 to 63, as said below
- apply_map: int32 [224, 2], replicated, may hold values from 0 to 63, as said below
- gram_old: bfloat16 [8, 64, 2, 512, 512], P('dp', 'fsdp'), may hold values from -59.73638 to 919.89638, as said below
- old_vectors: bfloat16 [8, 64, 2, 512, 512], P('dp', 'fsdp'), may hold values from -1 to 1
Outputs:
- eig_codes: bfloat16 [8, 64, 2, 512, 512], P('dp', 'fsdp')
- eig_scales: bfloat16 [8, 64, 2, 512, 8], P('dp', 'fsdp')
The draws below stay inside these ranges and needn't reach their ends.
Inputs may be any that keep to these rules, and one draw needn't show every extreme that they name: `owner_map`: within one dp index (blocks e * 28 to e * 28 + 27) no two blocks share an owner, and of the fsdp indices f and f + 32 at most one owns a block of it. `apply_map`: within one dp index each fsdp index receives at most 2 of the 56 factors, and some fsdp index receives exactly 2 in every dp index. `gram_old`: each [512, 512] matrix is symmetric.
All inputs are finite; a program needn't handle non-finite values. Where the reference program divides by a largest or mean magnitude, that divisor is 1e-20 or more.
Results may differ from the reference program's by a relative error of at most 0.017.
Values may be sent and summed in bfloat16 or wider, within the bound.
A program may use at most 64 MiB of HBM per device.

```python
import math
import jax
import jax.numpy as jnp
from jax import lax

BS = 512
QG = 64
ITERS = 2
AP_CAP = 2
NB_DP = 28
NBLK = 224
N_DP = 8
N_FSDP = 64


def draw_grad_parts(key, part):
    key = jax.random.fold_in(key, 11)
    full_shape = (N_DP, NBLK, BS, BS)
    values = jnp.clip(jax.random.normal(key, full_shape, jnp.float32), -4.0, 4.0)
    return values.astype(jnp.bfloat16)


def draw_owner_map(key, part):
    key = jax.random.fold_in(key, 12)

    def one_range(range_key):
        pair_key, half_key = jax.random.split(range_key)
        pair_ids = jax.random.permutation(pair_key, N_FSDP // 2)[:NB_DP].astype(jnp.int32)
        halves = jax.random.randint(half_key, (NB_DP,), 0, 2).astype(jnp.int32)
        return pair_ids + halves * (N_FSDP // 2)
    return jax.vmap(one_range)(jax.random.split(key, N_DP)).reshape(NBLK).astype(jnp.int32)


def draw_apply_map(key, part):
    key = jax.random.fold_in(key, 13)
    total = 2 * NB_DP

    def one_range(range_key):
        count_key, rank_key, order_key = jax.random.split(range_key, 3)
        doubled = jax.random.randint(count_key, (), 1, total // AP_CAP + 1).astype(jnp.int32)
        rank_ids = jax.random.permutation(rank_key, N_FSDP).astype(jnp.int32)
        places = jnp.arange(total, dtype=jnp.int32)
        second = jnp.clip(places - (AP_CAP - 1) * doubled, 0, N_FSDP - 1)
        chosen = jnp.where(places < AP_CAP * doubled, rank_ids[places // AP_CAP], rank_ids[second])
        shuffle = jax.random.permutation(order_key, total)
        return chosen[shuffle]
    return jax.vmap(one_range)(jax.random.split(key, N_DP)).reshape(NBLK, 2).astype(jnp.int32)


def draw_gram_old(key, part):
    key = jax.random.fold_in(key, 14)
    unit_size = BS * N_DP
    full_shape = (N_DP, N_FSDP, 2, BS, BS)
    noise = jax.random.uniform(key, full_shape, jnp.float32, -1.0, 1.0)
    spread = 0.13 * unit_size / math.sqrt(BS)
    symmetric = (noise + jnp.swapaxes(noise, 3, 4)) * (spread / math.sqrt(2.0))
    return (symmetric + 0.2 * unit_size * jnp.eye(BS, dtype=jnp.float32)).astype(jnp.bfloat16)


def draw_old_vectors(key, part):
    key = jax.random.fold_in(key, 15)
    levels = BS.bit_length() - 1

    def one_matrix(matrix_key):
        rotate_key, noise_key = jax.random.split(matrix_key)
        current = jnp.eye(BS, dtype=jnp.float32)
        for section_index in range(levels):
            stride = 2 ** section_index
            angles = jax.random.uniform(jax.random.fold_in(rotate_key, section_index), (BS // (2 * stride), 1, stride, 1), jnp.float32, -math.pi, math.pi)
            paired = current.reshape(BS // (2 * stride), 2, stride, BS)
            top_half = paired[:, 0:1]
            low_half = paired[:, 1:2]
            cosine = jnp.cos(angles)
            sine_value = jnp.sin(angles)
            current = jnp.concatenate([cosine * top_half - sine_value * low_half, sine_value * top_half + cosine * low_half], axis=1).reshape(BS, BS)
        drifted = current + jax.random.normal(noise_key, (BS, BS), jnp.float32) * (0.3 / math.sqrt(BS))
        return jnp.clip(drifted, -1.0, 1.0)
    matrices = lax.map(one_matrix, jax.random.split(key, N_DP * N_FSDP * 2))
    return matrices.reshape(N_DP, N_FSDP, 2, BS, BS).astype(jnp.bfloat16)


def setup_inputs(seed: int = 0) -> dict:
    key_list = jax.random.split(jax.random.key(seed), 6)
    grad_parts = draw_grad_parts(jax.random.fold_in(key_list[5], 71), 0)
    owner_map = draw_owner_map(jax.random.fold_in(key_list[5], 71), 0)
    apply_map = draw_apply_map(jax.random.fold_in(key_list[5], 71), 0)
    gram_old = draw_gram_old(jax.random.fold_in(key_list[5], 71), 0)
    old_vectors = draw_old_vectors(jax.random.fold_in(key_list[5], 71), 0)
    return dict(grad_parts=grad_parts, owner_map=owner_map, apply_map=apply_map, gram_old=gram_old, old_vectors=old_vectors)


ema_decay = 0.95
norm_eps = 1e-06

def quantize(iterate):
    grouped = iterate.reshape(BS, BS // QG, QG)
    group_scale = (lax.optimization_barrier(jnp.max(jnp.abs(grouped), axis=2)) + norm_eps).astype(jnp.bfloat16)
    code_tiles = (grouped / group_scale.astype(jnp.float32)[:, :, None]).astype(jnp.bfloat16)
    return (code_tiles.reshape(BS, BS), group_scale)

def refresh(side_matrix, old_state, old_basis):
    gram_sum = jnp.dot(side_matrix, side_matrix.T, preferred_element_type=jnp.float32)
    ema_state = ema_decay * old_state.astype(jnp.float32) + (1.0 - ema_decay) * gram_sum
    projected = jnp.dot(ema_state, old_basis.astype(jnp.float32), precision=lax.Precision.HIGHEST)
    iterate = projected / jnp.sqrt(lax.optimization_barrier(jnp.sum(projected * projected, axis=0, keepdims=True)) + norm_eps)
    for sweep_index in range(ITERS):
        inner_gram = jnp.dot(iterate.T, iterate, precision=lax.Precision.HIGHEST)
        iterate = 1.5 * iterate - 0.5 * jnp.dot(iterate, inner_gram, precision=lax.Precision.HIGHEST)
    return quantize(iterate)

def reference(grad_parts, owner_map, apply_map, gram_old, old_vectors):
    gradient = lax.optimization_barrier(jnp.sum(grad_parts, axis=0, dtype=jnp.float32)).astype(jnp.bfloat16)

    def one_block(block_index):
        side_matrix = gradient[block_index]
        range_index = block_index // NB_DP
        owner_rank = owner_map[block_index]
        states = gram_old[range_index, owner_rank]
        old_bases = old_vectors[range_index, owner_rank]
        left_side = refresh(side_matrix, states[0], old_bases[0])
        right_side = refresh(side_matrix.T, states[1], old_bases[1])
        return (jnp.stack([left_side[0], right_side[0]]), jnp.stack([left_side[1], right_side[1]]))
    code_tiles, scales = lax.map(one_block, jnp.arange(NBLK, dtype=jnp.int32))
    apply_ranks = apply_map.reshape(N_DP, 2 * NB_DP)
    factor_ids = jnp.arange(2 * NB_DP, dtype=jnp.int32)
    same_rank = apply_ranks[:, :, None] == apply_ranks[:, None, :]
    earlier = factor_ids[None, :] < factor_ids[:, None]
    slot_index = lax.optimization_barrier(jnp.sum((same_rank & earlier[None]).astype(jnp.int32), axis=2))
    range_ids = jnp.broadcast_to(jnp.arange(N_DP, dtype=jnp.int32)[:, None], (N_DP, 2 * NB_DP))
    eig_codes = jnp.zeros((N_DP, N_FSDP, AP_CAP, BS, BS), jnp.bfloat16)
    eig_codes = eig_codes.at[range_ids, apply_ranks, slot_index].set(code_tiles.reshape(N_DP, 2 * NB_DP, BS, BS))
    eig_scales = jnp.zeros((N_DP, N_FSDP, AP_CAP, BS, BS // QG), jnp.bfloat16)
    eig_scales = eig_scales.at[range_ids, apply_ranks, slot_index].set(scales.reshape(N_DP, 2 * NB_DP, BS, BS // QG))
    return (eig_codes, eig_scales)
```

```python
import functools

import jax
import jax.numpy as jnp
from jax import lax
from jax.experimental import pallas as pl
from jax.experimental.pallas import tpu as pltpu
from jax.sharding import PartitionSpec as P

QG = 64
ITERS = 2
AP_CAP = 2
MESH = pl.DeviceIdType.MESH

ema_decay = 0.95
norm_eps = 1e-06

N_CHUNK = 4
F32 = jnp.float32
BF16 = jnp.bfloat16


def dot_nn(a, b):
    return jnp.dot(a, b, preferred_element_type=F32)


def dot_nt(a, b):
    return lax.dot_general(a, b, (((1,), (1,)), ((), ())), preferred_element_type=F32)


def split(value):
    high = value.astype(BF16)
    return high, (value - high.astype(F32)).astype(BF16)


def wait_bytes(ref, sem):
    pltpu.make_async_copy(ref, ref, sem).wait()


def kernel(
    n_dp, n_fsdp, per_range,
    table, grads, grams, vectors,
    codes_out, scales_out,
    grad_v, sums_up, sums_down, summed, outgoing, stripes,
    gram_own, vec_own, gram_far, vec_far, iterate_m, held, chosen, landed, scale_m,
    load_sem, far_send, far_recv, up_send, up_recv, down_send, down_recv,
    first_send, first_recv, second_send, second_recv, third_send, third_recv,
):
    dp = lax.axis_index("dp")
    me = lax.axis_index("fsdp")
    half_count = n_fsdp // 2
    side = me // half_count
    extent = gram_own.shape[0]
    width = extent // N_CHUNK
    piece_rows, piece_cols = held.shape[1], held.shape[2]
    group = 8

    loads = [
        pltpu.make_async_copy(grads, grad_v, load_sem.at[0]),
        pltpu.make_async_copy(grams.at[side], gram_own, load_sem.at[1]),
        pltpu.make_async_copy(vectors.at[side], vec_own, load_sem.at[2]),
    ]
    for load in loads:
        load.start()

    barrier = pltpu.get_barrier_semaphore()

    def greet(k, carry):
        pl.semaphore_signal(barrier, inc=1, device_id={"fsdp": me ^ k}, device_id_type=MESH)
        return carry

    up = lax.rem(dp + 1, n_dp)
    down = lax.rem(dp + n_dp - 1, n_dp)
    pl.semaphore_signal(barrier, inc=1, device_id={"dp": up}, device_id_type=MESH)
    pl.semaphore_signal(barrier, inc=1, device_id={"dp": down}, device_id_type=MESH)
    lax.fori_loop(1, n_fsdp, greet, 0)
    pl.semaphore_wait(barrier, n_fsdp + 1)

    mate = lax.rem(me + half_count, n_fsdp)
    n_band = 4
    band = extent // n_band
    swaps = [
        pltpu.make_async_remote_copy(
            src_ref=vectors.at[1 - side], dst_ref=vec_far,
            send_sem=far_send.at[n_band], recv_sem=far_recv.at[n_band],
            device_id={"fsdp": mate}, device_id_type=MESH,
        )
    ]
    for i in range(n_band):
        rows, cols = pl.ds(i * band, band), pl.ds(i * band, extent - i * band)
        swaps.append(
            pltpu.make_async_remote_copy(
                src_ref=grams.at[1 - side, rows, cols], dst_ref=gram_far.at[rows, cols],
                send_sem=far_send.at[i], recv_sem=far_recv.at[i],
                device_id={"fsdp": mate}, device_id_type=MESH,
            )
        )

    half = per_range // 2
    far_off = n_dp // 2
    ways = (
        (1, up, sums_up, up_send, up_recv, pl.ds(0, half)),
        (-1, down, sums_down, down_send, down_recv, pl.ds(half, per_range - half)),
    )

    def columns(c):
        return pl.ds(c * width, width)

    def ring_copy(way, c, step):
        sign, target, sums, send, recv, part = way
        dest = lax.rem(dp + sign * (far_off - step) + n_dp, n_dp)
        if step == 0:
            src = grad_v.at[dest, part, :, columns(c)]
            dst = sums.at[0, part, :, columns(c)]
        else:
            src = sums.at[step - 1, :, :, columns(c)]
            dst = sums.at[step, :, :, columns(c)]
        return pltpu.make_async_remote_copy(
            src_ref=src, dst_ref=dst, send_sem=send.at[c, step], recv_sem=recv.at[c, step],
            device_id={"dp": target}, device_id_type=MESH,
        )

    def ring_step(c, step):
        for way in ways:
            sign, target, sums, send, recv, part = way
            if step > 0:
                ring_copy(way, c, step - 1).wait_recv()
                dest = lax.rem(dp + sign * (far_off - step) + n_dp, n_dp)
                if step == 1:
                    other = pl.ds(half, per_range - half) if sign == 1 else pl.ds(0, half)
                    sums[0, part, :, columns(c)] = (
                        sums[0, part, :, columns(c)].astype(F32)
                        + grad_v[dest, part, :, columns(c)].astype(F32)
                    ).astype(BF16)
                    sums[0, other, :, columns(c)] = grad_v[dest, other, :, columns(c)]
                else:
                    sums[step - 1, :, :, columns(c)] = (
                        sums[step - 1, :, :, columns(c)].astype(F32)
                        + grad_v[dest, :, :, columns(c)].astype(F32)
                    ).astype(BF16)
            ring_copy(way, c, step).start()

    def finish(c):
        for way in ways:
            ring_copy(way, c, far_off - 1).wait_recv()
        total = (
            grad_v[dp, :, :, columns(c)].astype(F32)
            + sums_up[far_off - 1, :, :, columns(c)].astype(F32)
            + sums_down[far_off - 1, :, :, columns(c)].astype(F32)
        )
        summed[c] = total.astype(BF16)

        def pick(p, carry):
            outgoing[c, p] = summed[c, table[p]]
            return carry

        lax.fori_loop(0, half_count, pick, 0)

        def post(k, carry):
            target = me ^ k
            pltpu.make_async_remote_copy(
                src_ref=outgoing.at[c, lax.rem(target, half_count)],
                dst_ref=stripes.at[me, :, columns(c)],
                send_sem=first_send, recv_sem=first_recv.at[c],
                device_id={"fsdp": target}, device_id_type=MESH,
            ).start()
            return carry

        lax.fori_loop(1, n_fsdp, post, 0)
        stripes[me, :, columns(c)] = outgoing[c, lax.rem(me, half_count)]

    loads[0].wait()
    for c in range(N_CHUNK):
        ring_step(c, 0)
    for swap in swaps:
        swap.start()
    order = sorted(
        (2 * c + step, -step, c, step) for c in range(N_CHUNK) for step in range(1, far_off + 1)
    )
    for _, _, c, step in order:
        if step < far_off:
            ring_step(c, step)
        else:
            finish(c)

    loads[1].wait()
    loads[2].wait()
    for swap in swaps:
        swap.wait_recv()
    owns = table[half_count + AP_CAP * n_fsdp] > 0
    basis = jnp.where(owns, vec_own[...], vec_far[...]).T
    for i in range(n_band):
        for j in range(i, n_band):
            rows, cols = pl.ds(i * band, band), pl.ds(j * band, band)
            tile = jnp.where(owns, gram_own[rows, cols], gram_far[rows, cols])
            gram_own[rows, cols] = tile
            if j > i:
                gram_own[cols, rows] = tile.T
    for c in range(N_CHUNK):
        wait_bytes(stripes.at[pl.ds(0, n_fsdp - 1), :, columns(c)], first_recv.at[c])
    block = stripes[...].astype(F32).reshape(extent, extent)

    @pl.when(side == 0)
    def _():
        iterate_m[...] = block.astype(BF16)

    @pl.when(side == 1)
    def _():
        iterate_m[...] = block.T.astype(BF16)

    matrix = iterate_m[...]
    state = ema_decay * gram_own[...].astype(F32) + (1.0 - ema_decay) * dot_nt(matrix, matrix)
    state_high, state_low = split(state)
    turned = dot_nn(basis, state_high) + dot_nn(basis, state_low)
    turned = turned / jnp.sqrt(jnp.sum(turned * turned, axis=1, keepdims=True) + norm_eps)
    for _ in range(ITERS):
        high, low = split(turned)
        inner = dot_nt(high, high) + dot_nt(high, low) + dot_nt(low, high)
        inner_high, inner_low = split(inner)
        turned = 1.5 * turned - 0.5 * (
            dot_nn(inner_high, high) + dot_nn(inner_high, low) + dot_nn(inner_low, high)
        )
    iterate_m[...] = turned.T.astype(BF16)

    def piece(i):
        return (
            pl.ds(pl.multiple_of((i // 2) * piece_rows, piece_rows), piece_rows),
            pl.ds(pl.multiple_of(lax.rem(i, 2) * piece_cols, piece_cols), piece_cols),
        )

    def spread(k, carry):
        target = me ^ k
        pltpu.make_async_remote_copy(
            src_ref=iterate_m.at[piece(target)], dst_ref=held.at[me],
            send_sem=second_send, recv_sem=second_recv,
            device_id={"fsdp": target}, device_id_type=MESH,
        ).start()
        return carry

    lax.fori_loop(1, n_fsdp, spread, 0)
    held[me] = iterate_m[piece(me)]
    held[n_fsdp] = jnp.zeros((piece_rows, piece_cols), BF16)
    wait_bytes(held.at[pl.ds(0, n_fsdp - 1)], second_recv)

    def select(target, place):
        for t in range(AP_CAP):
            place[target, t] = held[table[half_count + t * n_fsdp + target]]

    def deliver(k, carry):
        target = me ^ k
        select(target, chosen)
        pltpu.make_async_remote_copy(
            src_ref=chosen.at[target], dst_ref=landed.at[me],
            send_sem=third_send, recv_sem=third_recv.at[k // group],
            device_id={"fsdp": target}, device_id_type=MESH,
        ).start()
        return carry

    lax.fori_loop(1, n_fsdp, deliver, 0)
    select(me, landed)

    lane = lax.broadcasted_iota(jnp.int32, (piece_rows, 128), 1)

    def quantize(m, carry):
        pair = (me // 2) ^ m
        rows = pl.ds(pl.multiple_of(pair * piece_rows, piece_rows), piece_rows)
        for t in range(AP_CAP):
            filled = table[half_count + t * n_fsdp + me] < n_fsdp
            scales = jnp.zeros((piece_rows, 128), F32)
            for h in range(2):
                for q in range(piece_cols // 128):
                    value = landed[2 * pair + h, t, :, pl.ds(q * 128, 128)].astype(F32)
                    size = jnp.abs(value)
                    first = jnp.max(jnp.where(lane < QG, size, 0.0), axis=1, keepdims=True)
                    last = jnp.max(jnp.where(lane < QG, 0.0, size), axis=1, keepdims=True)
                    first = (first + norm_eps).astype(BF16).astype(F32)
                    last = (last + norm_eps).astype(BF16).astype(F32)
                    code = value / jnp.where(lane < QG, first, last)
                    at = h * piece_cols + q * 128
                    codes_out[t, rows, pl.ds(at, 128)] = code.astype(BF16)
                    place = at // QG
                    scales = jnp.where(lane == place, first, scales)
                    scales = jnp.where(lane == place + 1, last, scales)
            scale_m[t, rows, :] = jnp.where(filled, scales, 0.0)
        return carry

    for g in range(n_fsdp // group):
        count = group - 1 if g == 0 else group
        wait_bytes(landed.at[pl.ds(0, count)], third_recv.at[g])
        lax.fori_loop(g * group // 2, (g + 1) * group // 2, quantize, 0)
    n_group = extent // QG
    for t in range(AP_CAP):
        scales_out[t] = scale_m[t].T[:n_group].astype(BF16)

    for swap in swaps:
        swap.wait_send()
    for c in range(N_CHUNK):
        for step in range(far_off):
            for way in ways:
                ring_copy(way, c, step).wait_send()
    for c in range(N_CHUNK):
        wait_bytes(stripes.at[pl.ds(0, n_fsdp - 1), :, columns(c)], first_send)
    wait_bytes(held.at[pl.ds(0, n_fsdp - 1)], second_send)
    wait_bytes(landed.at[pl.ds(0, n_fsdp - 1)], third_send)


def make_table(owner_map, apply_map, n_dp, n_fsdp):
    per_range = owner_map.shape[0] // n_dp
    half_count = n_fsdp // 2
    dp = lax.axis_index("dp")
    me = lax.axis_index("fsdp")
    owners = lax.dynamic_slice_in_dim(owner_map, dp * per_range, per_range)
    ranks = lax.dynamic_slice_in_dim(apply_map, dp * per_range, per_range).reshape(2 * per_range)
    pairs = owners % half_count
    at_pair = pairs[None, :] == jnp.arange(half_count, dtype=jnp.int32)[:, None]
    block_of = jnp.sum(
        jnp.where(at_pair, jnp.arange(per_range, dtype=jnp.int32)[None, :], 0), axis=1
    )
    sources = (
        pairs[:, None] + half_count * jnp.arange(2, dtype=jnp.int32)[None, :]
    ).reshape(2 * per_range)
    ids = jnp.arange(2 * per_range, dtype=jnp.int32)
    slots = jnp.sum(
        ((ranks[:, None] == ranks[None, :]) & (ids[None, :] < ids[:, None])).astype(jnp.int32),
        axis=1,
    )
    places = slots * n_fsdp + ranks
    wanted = places[None, :] == jnp.arange(AP_CAP * n_fsdp, dtype=jnp.int32)[:, None]
    select = n_fsdp - jnp.sum(jnp.where(wanted, n_fsdp - sources[None, :], 0), axis=1)
    owns = jnp.any(owners == me).astype(jnp.int32)
    return jnp.concatenate([block_of, select, owns[None]]).astype(jnp.int32)


def local(grad_parts, owner_map, apply_map, gram_old, old_vectors):
    n_dp = lax.axis_size("dp")
    n_fsdp = lax.axis_size("fsdp")
    per_range = owner_map.shape[0] // n_dp
    stripe, extent = grad_parts.shape[2], grad_parts.shape[3]
    table = make_table(owner_map, apply_map, n_dp, n_fsdp)
    grads = grad_parts.reshape(n_dp, per_range, stripe, extent)
    far_off = n_dp // 2
    width = extent // N_CHUNK
    piece = (extent * 2 // n_fsdp, extent // 2)
    vmem, dma = pltpu.VMEM, pltpu.SemaphoreType.DMA
    codes, scales = pl.pallas_call(
        functools.partial(kernel, n_dp, n_fsdp, per_range),
        out_shape=(
            jax.ShapeDtypeStruct((AP_CAP, extent, extent), BF16),
            jax.ShapeDtypeStruct((AP_CAP, extent // QG, extent), BF16),
        ),
        in_specs=[pl.BlockSpec(memory_space=pltpu.SMEM)] + [pl.BlockSpec(memory_space=pl.ANY)] * 3,
        out_specs=(pl.BlockSpec(memory_space=pltpu.VMEM), pl.BlockSpec(memory_space=pltpu.VMEM)),
        scratch_shapes=[
            vmem((n_dp, per_range, stripe, extent), BF16),
            vmem((far_off, per_range, stripe, extent), BF16),
            vmem((far_off, per_range, stripe, extent), BF16),
            vmem((N_CHUNK, per_range, stripe, width), BF16),
            vmem((N_CHUNK, n_fsdp // 2, stripe, width), BF16),
            vmem((n_fsdp, stripe, extent), BF16),
            vmem((extent, extent), BF16),
            vmem((extent, extent), BF16),
            vmem((extent, extent), BF16),
            vmem((extent, extent), BF16),
            vmem((extent, extent), BF16),
            vmem((n_fsdp + 1,) + piece, BF16),
            vmem((n_fsdp, AP_CAP) + piece, BF16),
            vmem((n_fsdp, AP_CAP) + piece, BF16),
            vmem((AP_CAP, extent, 128), F32),
            dma((3,)),
            dma((5,)), dma((5,)),
            dma((N_CHUNK, far_off)), dma((N_CHUNK, far_off)),
            dma((N_CHUNK, far_off)), dma((N_CHUNK, far_off)),
            dma, dma((N_CHUNK,)),
            dma, dma,
            dma, dma((n_fsdp // 8,)),
        ],
        compiler_params=pltpu.CompilerParams(
            collective_id=0, has_side_effects=True, vmem_limit_bytes=48 * 2**20
        ),
        name="refresh",
    )(table, grads, gram_old[0, 0], old_vectors[0, 0])
    return codes[None, None], jnp.swapaxes(scales, 1, 2)[None, None]


def solution(mesh):
    placed = (
        P("dp", None, "fsdp", None),
        P(),
        P(),
        P("dp", "fsdp", None, None, None),
        P("dp", "fsdp", None, None, None),
    )
    return jax.shard_map(
        local,
        mesh=mesh,
        in_specs=placed,
        out_specs=(P("dp", "fsdp", None, None, None), P("dp", "fsdp", None, None, None)),
        check_vma=False,
    )
```

```python
import functools

import jax
import jax.numpy as jnp
from jax import lax
from jax.experimental import pallas as pl
from jax.experimental.pallas import tpu as pltpu
from jax.sharding import PartitionSpec as P

QG = 64
ITERS = 2
AP_CAP = 2
MESH = pl.DeviceIdType.MESH

ema_decay = 0.95
norm_eps = 1e-06

N_CHUNK = 4
F32 = jnp.float32
BF16 = jnp.bfloat16


def dot_nn(a, b):
    return jnp.dot(a, b, preferred_element_type=F32)


def dot_nt(a, b):
    return lax.dot_general(a, b, (((1,), (1,)), ((), ())), preferred_element_type=F32)


def split(value):
    high = value.astype(BF16)
    return high, (value - high.astype(F32)).astype(BF16)


def wait_bytes(ref, sem):
    pltpu.make_async_copy(ref, ref, sem).wait()


def kernel(
    n_dp, n_fsdp, per_range,
    owner_map, apply_map, grads, grams, vectors,
    codes_out, scales_out,
    owner_v, apply_v, table_v, table,
    grad_v, sums_up, sums_down, summed, outgoing, stripes,
    gram_own, vec_own, gram_far, vec_far, iterate_m, held_upper, held_lower, chosen, landed, scale_m,
    load_sem, far_send, far_recv, up_send, up_recv, down_send, down_recv,
    first_send, first_recv, second_send, second_recv, third_send, third_recv,
):
    dp = lax.axis_index("dp")
    me = lax.axis_index("fsdp")
    half_count = n_fsdp // 2
    side = me // half_count
    extent = gram_own.shape[0]
    width = extent // N_CHUNK
    held = (held_upper, held_lower)
    piece_rows, piece_cols = held_upper.shape[1:]
    across = extent // piece_cols
    group = 8

    loads = [
        pltpu.make_async_copy(grads, grad_v, load_sem.at[0]),
        pltpu.make_async_copy(grams.at[side], gram_own, load_sem.at[1]),
        pltpu.make_async_copy(vectors.at[side], vec_own, load_sem.at[2]),
        pltpu.make_async_copy(owner_map, owner_v, load_sem.at[3]),
        pltpu.make_async_copy(apply_map, apply_v, load_sem.at[4]),
    ]
    for load in loads:
        load.start()

    barrier = pltpu.get_barrier_semaphore()

    def greet(k, carry):
        pl.semaphore_signal(barrier, inc=1, device_id={"fsdp": me ^ k}, device_id_type=MESH)
        return carry

    up = lax.rem(dp + 1, n_dp)
    down = lax.rem(dp + n_dp - 1, n_dp)
    pl.semaphore_signal(barrier, inc=1, device_id={"dp": up}, device_id_type=MESH)
    pl.semaphore_signal(barrier, inc=1, device_id={"dp": down}, device_id_type=MESH)
    lax.fori_loop(1, n_fsdp, greet, 0)
    loads[3].wait()
    loads[4].wait()
    fill_table(dp, me, half_count, per_range, owner_v, apply_v, table_v)
    to_scalars = pltpu.make_async_copy(table_v, table, load_sem.at[5])
    to_scalars.start()
    pl.semaphore_wait(barrier, n_fsdp + 1)

    mate = lax.rem(me + half_count, n_fsdp)
    n_band = 4
    band = extent // n_band
    swaps = [
        pltpu.make_async_remote_copy(
            src_ref=vectors.at[1 - side], dst_ref=vec_far,
            send_sem=far_send.at[n_band], recv_sem=far_recv.at[n_band],
            device_id={"fsdp": mate}, device_id_type=MESH,
        )
    ]
    for i in range(n_band):
        rows, cols = pl.ds(i * band, band), pl.ds(i * band, extent - i * band)
        swaps.append(
            pltpu.make_async_remote_copy(
                src_ref=grams.at[1 - side, rows, cols], dst_ref=gram_far.at[rows, cols],
                send_sem=far_send.at[i], recv_sem=far_recv.at[i],
                device_id={"fsdp": mate}, device_id_type=MESH,
            )
        )

    half = per_range // 2
    far_off = n_dp // 2
    ways = (
        (1, up, sums_up, up_send, up_recv, pl.ds(0, half)),
        (-1, down, sums_down, down_send, down_recv, pl.ds(half, per_range - half)),
    )

    def columns(c):
        return pl.ds(c * width, width)

    def ring_copy(way, c, step):
        sign, target, sums, send, recv, part = way
        dest = lax.rem(dp + sign * (far_off - step) + n_dp, n_dp)
        if step == 0:
            src = grad_v.at[dest, part, :, columns(c)]
            dst = sums.at[0, part, :, columns(c)]
        else:
            src = sums.at[step - 1, :, :, columns(c)]
            dst = sums.at[step, :, :, columns(c)]
        return pltpu.make_async_remote_copy(
            src_ref=src, dst_ref=dst, send_sem=send.at[c, step], recv_sem=recv.at[c, step],
            device_id={"dp": target}, device_id_type=MESH,
        )

    def ring_step(c, step):
        for way in ways:
            sign, target, sums, send, recv, part = way
            if step > 0:
                ring_copy(way, c, step - 1).wait_recv()
                dest = lax.rem(dp + sign * (far_off - step) + n_dp, n_dp)
                if step == 1:
                    other = pl.ds(half, per_range - half) if sign == 1 else pl.ds(0, half)
                    sums[0, part, :, columns(c)] = (
                        sums[0, part, :, columns(c)].astype(F32)
                        + grad_v[dest, part, :, columns(c)].astype(F32)
                    ).astype(BF16)
                    sums[0, other, :, columns(c)] = grad_v[dest, other, :, columns(c)]
                else:
                    sums[step - 1, :, :, columns(c)] = (
                        sums[step - 1, :, :, columns(c)].astype(F32)
                        + grad_v[dest, :, :, columns(c)].astype(F32)
                    ).astype(BF16)
            ring_copy(way, c, step).start()

    def finish(c):
        for way in ways:
            ring_copy(way, c, far_off - 1).wait_recv()
        total = (
            grad_v[dp, :, :, columns(c)].astype(F32)
            + sums_up[far_off - 1, :, :, columns(c)].astype(F32)
            + sums_down[far_off - 1, :, :, columns(c)].astype(F32)
        )
        summed[c] = total.astype(BF16)

        def pick(p, carry):
            outgoing[c, p] = summed[c, table[p, 2]]
            return carry

        lax.fori_loop(0, half_count, pick, 0)

        def post(k, carry):
            target = me ^ k
            pltpu.make_async_remote_copy(
                src_ref=outgoing.at[c, lax.rem(target, half_count)],
                dst_ref=stripes.at[me, :, columns(c)],
                send_sem=first_send, recv_sem=first_recv.at[c],
                device_id={"fsdp": target}, device_id_type=MESH,
            ).start()
            return carry

        lax.fori_loop(1, n_fsdp, post, 0)
        stripes[me, :, columns(c)] = outgoing[c, lax.rem(me, half_count)]

    loads[0].wait()
    for c in range(N_CHUNK):
        ring_step(c, 0)
    to_scalars.wait()
    for swap in swaps:
        swap.start()
    order = sorted(
        (0.5 * c + step, -step, c, step) for c in range(N_CHUNK) for step in range(1, far_off + 1)
    )
    for _, _, c, step in order:
        if step < far_off:
            ring_step(c, step)
        else:
            finish(c)

    loads[1].wait()
    loads[2].wait()
    for swap in swaps:
        swap.wait_recv()
    owns = table[0, 3] > 0
    basis = jnp.where(owns, vec_own[...], vec_far[...]).T
    for i in range(n_band):
        for j in range(i, n_band):
            rows, cols = pl.ds(i * band, band), pl.ds(j * band, band)
            tile = jnp.where(owns, gram_own[rows, cols], gram_far[rows, cols])
            gram_own[rows, cols] = tile
            if j > i:
                gram_own[cols, rows] = tile.T
    for c in range(N_CHUNK):
        wait_bytes(stripes.at[pl.ds(0, n_fsdp - 1), :, columns(c)], first_recv.at[c])
    block = stripes[...].astype(F32).reshape(extent, extent)

    @pl.when(side == 0)
    def _():
        iterate_m[...] = block.astype(BF16)

    @pl.when(side == 1)
    def _():
        iterate_m[...] = block.T.astype(BF16)

    matrix = iterate_m[...]
    state = ema_decay * gram_own[...].astype(F32) + (1.0 - ema_decay) * dot_nt(matrix, matrix)
    state_high, state_low = split(state)
    turned = dot_nn(basis, state_high) + dot_nn(basis, state_low)
    turned = turned / jnp.sqrt(jnp.sum(turned * turned, axis=1, keepdims=True) + norm_eps)
    for _ in range(ITERS - 1):
        high, low = split(turned)
        inner_high, inner_low = split(dot_nt(high, high) + dot_nt(high, low) + dot_nt(low, high))
        turned = 1.5 * turned - 0.5 * (
            dot_nn(inner_high, high) + dot_nn(inner_high, low) + dot_nn(inner_low, high)
        )
    high, low = split(turned)
    inner_high, inner_low = split(dot_nt(high, high) + dot_nt(high, low) + dot_nt(low, high))

    half_rows = extent // 2

    def piece(h, i):
        row = h * half_rows + (i // across) * piece_rows
        col = lax.rem(i, across) * piece_cols
        return (
            pl.ds(pl.multiple_of(row, piece_rows), piece_rows),
            pl.ds(pl.multiple_of(col, piece_cols), piece_cols),
        )

    for h in range(2):
        part = slice(h * half_rows, (h + 1) * half_rows)
        last = 1.5 * turned[:, part] - 0.5 * (
            dot_nn(inner_high, high[:, part])
            + dot_nn(inner_high, low[:, part])
            + dot_nn(inner_low, high[:, part])
        )
        iterate_m[pl.ds(h * half_rows, half_rows), :] = last.T.astype(BF16)

        def spread(k, carry):
            target = me ^ k
            pltpu.make_async_remote_copy(
                src_ref=iterate_m.at[piece(h, target)], dst_ref=held[h].at[me],
                send_sem=second_send, recv_sem=second_recv.at[h],
                device_id={"fsdp": target}, device_id_type=MESH,
            ).start()
            return carry

        lax.fori_loop(1, n_fsdp, spread, 0)
        held[h][me] = iterate_m[piece(h, me)]
        held[h][n_fsdp] = jnp.zeros((piece_rows, piece_cols), BF16)

    def select(h, target, place):
        for t in range(AP_CAP):
            place[h, target, t] = held[h][table[target, t]]

    for h in range(2):
        wait_bytes(held[h].at[pl.ds(0, n_fsdp - 1)], second_recv.at[h])

        def deliver(k, carry):
            target = me ^ k
            select(h, target, chosen)
            pltpu.make_async_remote_copy(
                src_ref=chosen.at[h, target], dst_ref=landed.at[h, me],
                send_sem=third_send, recv_sem=third_recv.at[h, k // group],
                device_id={"fsdp": target}, device_id_type=MESH,
            ).start()
            return carry

        lax.fori_loop(1, n_fsdp, deliver, 0)
        for t in range(AP_CAP):
            landed[h, me, t] = held[h][table[me, t]]

    lane = lax.broadcasted_iota(jnp.int32, (piece_rows, piece_cols), 1)

    def quantize(h, m):
        band_at = (me // across) ^ m
        rows = pl.ds(pl.multiple_of(h * half_rows + band_at * piece_rows, piece_rows), piece_rows)
        for t in range(AP_CAP):
            filled = table[me, t] < n_fsdp
            scales = jnp.zeros((piece_rows, 128), F32)
            for q in range(across):
                value = landed[h, across * band_at + q, t].astype(F32)
                size = jnp.abs(value)
                first = jnp.max(jnp.where(lane < QG, size, 0.0), axis=1, keepdims=True)
                last = jnp.max(jnp.where(lane < QG, 0.0, size), axis=1, keepdims=True)
                first = (first + norm_eps).astype(BF16).astype(F32)
                last = (last + norm_eps).astype(BF16).astype(F32)
                code = value / jnp.where(lane < QG, first, last)
                codes_out[t, rows, pl.ds(q * piece_cols, piece_cols)] = code.astype(BF16)
                scales = jnp.where(lane == 2 * q, first, scales)
                scales = jnp.where(lane == 2 * q + 1, last, scales)
            scale_m[t, rows, :] = jnp.where(filled, scales, 0.0)

    for h in range(2):
        for g in range(n_fsdp // group):
            count = group - 1 if g == 0 else group
            wait_bytes(landed.at[h, pl.ds(0, count)], third_recv.at[h, g])

            def several(m, carry):
                quantize(h, m)
                return carry

            lax.fori_loop(g * group // across, (g + 1) * group // across, several, 0)
    n_group = extent // QG
    for t in range(AP_CAP):
        scales_out[t] = scale_m[t].T[:n_group].astype(BF16)

    for swap in swaps:
        swap.wait_send()
    for c in range(N_CHUNK):
        for step in range(far_off):
            for way in ways:
                ring_copy(way, c, step).wait_send()
    for c in range(N_CHUNK):
        wait_bytes(stripes.at[pl.ds(0, n_fsdp - 1), :, columns(c)], first_send)
    for h in range(2):
        wait_bytes(held[h].at[pl.ds(0, n_fsdp - 1)], second_send)
        wait_bytes(landed.at[h, pl.ds(0, n_fsdp - 1)], third_send)


def fill_table(dp, me, half_count, per_range, owner_v, apply_v, table_v):
    n_fsdp = 2 * half_count
    shape = (n_fsdp, owner_v.shape[1])
    ids = lax.broadcasted_iota(jnp.int32, shape, 1) - dp * per_range
    ranks = lax.broadcasted_iota(jnp.int32, shape, 0)
    ours = (ids >= 0) & (ids < per_range)
    owners = jnp.broadcast_to(owner_v[...], shape)
    pairs = owners & (half_count - 1)
    none = 2 * per_range * n_fsdp
    first = jnp.full((n_fsdp, 1), none, jnp.int32)
    last = jnp.full((n_fsdp, 1), -1, jnp.int32)
    for s in range(2):
        hit = ours & (jnp.broadcast_to(apply_v[pl.ds(s, 1), :], shape) == ranks)
        key = (2 * ids + s) * n_fsdp + s * half_count + pairs
        first = jnp.minimum(first, jnp.min(jnp.where(hit, key, none), axis=1, keepdims=True))
        last = jnp.maximum(last, jnp.max(jnp.where(hit, key, -1), axis=1, keepdims=True))
    slot_0 = jnp.where(first < none, first & (n_fsdp - 1), n_fsdp)
    slot_1 = jnp.where(last > first, last & (n_fsdp - 1), n_fsdp)
    block = jnp.max(jnp.where(ours & (pairs == ranks), ids, 0), axis=1, keepdims=True)
    owns = jnp.max(jnp.where(ours & (owners == me), 1, 0), axis=1, keepdims=True)
    lane = lax.broadcasted_iota(jnp.int32, table_v.shape, 1)
    out = jnp.where(lane == 0, slot_0, slot_1)
    out = jnp.where(lane == 2, block, out)
    table_v[...] = jnp.where(lane == 3, owns, out)


def local(grad_parts, owner_map, apply_map, gram_old, old_vectors):
    n_dp = lax.axis_size("dp")
    n_fsdp = lax.axis_size("fsdp")
    per_range = owner_map.shape[0] // n_dp
    stripe, extent = grad_parts.shape[2], grad_parts.shape[3]
    grads = grad_parts.reshape(n_dp, per_range, stripe, extent)
    far_off = n_dp // 2
    width = extent // N_CHUNK
    piece = (extent * 2 // n_fsdp, extent // 4)
    vmem, dma = pltpu.VMEM, pltpu.SemaphoreType.DMA
    in_hbm = [
        pltpu.with_memory_space_constraint(value, pltpu.HBM)
        for value in (owner_map[None], apply_map.T, grads, gram_old[0, 0], old_vectors[0, 0])
    ]
    codes, scales = pl.pallas_call(
        functools.partial(kernel, n_dp, n_fsdp, per_range),
        out_shape=(
            jax.ShapeDtypeStruct((AP_CAP, extent, extent), BF16),
            jax.ShapeDtypeStruct((AP_CAP, extent // QG, extent), BF16),
        ),
        in_specs=[pl.BlockSpec(memory_space=pl.ANY)] * 5,
        out_specs=(pl.BlockSpec(memory_space=pltpu.VMEM), pl.BlockSpec(memory_space=pltpu.VMEM)),
        scratch_shapes=[
            vmem((1, owner_map.shape[0]), jnp.int32),
            vmem((2, owner_map.shape[0]), jnp.int32),
            vmem((n_fsdp, 128), jnp.int32),
            pltpu.SMEM((n_fsdp, 128), jnp.int32),
            vmem((n_dp, per_range, stripe, extent), BF16),
            vmem((far_off, per_range, stripe, extent), BF16),
            vmem((far_off, per_range, stripe, extent), BF16),
            vmem((N_CHUNK, per_range, stripe, width), BF16),
            vmem((N_CHUNK, n_fsdp // 2, stripe, width), BF16),
            vmem((n_fsdp, stripe, extent), BF16),
            vmem((extent, extent), BF16),
            vmem((extent, extent), BF16),
            vmem((extent, extent), BF16),
            vmem((extent, extent), BF16),
            vmem((extent, extent), BF16),
            vmem((n_fsdp + 1,) + piece, BF16),
            vmem((n_fsdp + 1,) + piece, BF16),
            vmem((2, n_fsdp, AP_CAP) + piece, BF16),
            vmem((2, n_fsdp, AP_CAP) + piece, BF16),
            vmem((AP_CAP, extent, 128), F32),
            dma((6,)),
            dma((5,)), dma((5,)),
            dma((N_CHUNK, far_off)), dma((N_CHUNK, far_off)),
            dma((N_CHUNK, far_off)), dma((N_CHUNK, far_off)),
            dma, dma((N_CHUNK,)),
            dma, dma((2,)),
            dma, dma((2, n_fsdp // 8)),
        ],
        compiler_params=pltpu.CompilerParams(
            collective_id=0, has_side_effects=True, vmem_limit_bytes=48 * 2**20
        ),
        name="refresh",
    )(*in_hbm)
    return codes[None, None], jnp.swapaxes(scales, 1, 2)[None, None]


def solution(mesh):
    placed = (
        P("dp", None, "fsdp", None),
        P(),
        P(),
        P("dp", "fsdp", None, None, None),
        P("dp", "fsdp", None, None, None),
    )
    return jax.shard_map(
        local,
        mesh=mesh,
        in_specs=placed,
        out_specs=(P("dp", "fsdp", None, None, None), P("dp", "fsdp", None, None, None)),
        check_vma=False,
    )
```

```python
import functools

import jax
import jax.numpy as jnp
from jax import lax
from jax.experimental import pallas as pl
from jax.experimental.pallas import tpu as pltpu
from jax.sharding import PartitionSpec as P

QG = 64
ITERS = 2
AP_CAP = 2
MESH = pl.DeviceIdType.MESH

ema_decay = 0.95
norm_eps = 1e-06

N_CHUNK = 4
F32 = jnp.float32
BF16 = jnp.bfloat16


def dot_nn(a, b):
    return jnp.dot(a, b, preferred_element_type=F32)


def dot_nt(a, b):
    return lax.dot_general(a, b, (((1,), (1,)), ((), ())), preferred_element_type=F32)


def split(value):
    high = value.astype(BF16)
    return high, (value - high.astype(F32)).astype(BF16)


def wait_bytes(ref, sem):
    pltpu.make_async_copy(ref, ref, sem).wait()


def kernel(
    n_dp, n_fsdp, per_range,
    owner_map, apply_map, grads, grams, vectors,
    codes_out, scales_out,
    owner_v, apply_v, table_v, table,
    grad_v, sums_up, sums_down, summed, outgoing, stripes,
    gram_own, vec_own, gram_far, vec_far, iterate_m, held_upper, held_lower, chosen, landed, scale_m,
    load_sem, far_send, far_recv, up_send, up_recv, down_send, down_recv,
    first_send, first_recv, second_send, second_recv, third_send, third_recv,
):
    dp = lax.axis_index("dp")
    me = lax.axis_index("fsdp")
    half_count = n_fsdp // 2
    side = me // half_count
    extent = gram_own.shape[0]
    width = extent // N_CHUNK
    held = (held_upper, held_lower)
    piece_rows, piece_cols = held_upper.shape[1:]
    across = extent // piece_cols
    group = 8

    loads = [
        pltpu.make_async_copy(grads, grad_v, load_sem.at[0]),
        pltpu.make_async_copy(grams.at[side], gram_own, load_sem.at[1]),
        pltpu.make_async_copy(vectors.at[side], vec_own, load_sem.at[2]),
        pltpu.make_async_copy(owner_map, owner_v, load_sem.at[3]),
        pltpu.make_async_copy(apply_map, apply_v, load_sem.at[4]),
    ]
    for load in loads:
        load.start()

    barrier = pltpu.get_barrier_semaphore()

    def greet(k, carry):
        pl.semaphore_signal(barrier, inc=1, device_id={"fsdp": me ^ k}, device_id_type=MESH)
        return carry

    up = lax.rem(dp + 1, n_dp)
    down = lax.rem(dp + n_dp - 1, n_dp)
    pl.semaphore_signal(barrier, inc=1, device_id={"dp": up}, device_id_type=MESH)
    pl.semaphore_signal(barrier, inc=1, device_id={"dp": down}, device_id_type=MESH)
    lax.fori_loop(1, n_fsdp, greet, 0)
    loads[3].wait()
    loads[4].wait()
    fill_table(dp, me, half_count, per_range, owner_v, apply_v, table_v)
    to_scalars = pltpu.make_async_copy(table_v, table, load_sem.at[5])
    to_scalars.start()
    pl.semaphore_wait(barrier, n_fsdp + 1)

    mate = lax.rem(me + half_count, n_fsdp)
    n_band = 4
    band = extent // n_band
    swaps = [
        pltpu.make_async_remote_copy(
            src_ref=vectors.at[1 - side], dst_ref=vec_far,
            send_sem=far_send.at[n_band], recv_sem=far_recv.at[n_band],
            device_id={"fsdp": mate}, device_id_type=MESH,
        )
    ]
    for i in range(n_band):
        rows, cols = pl.ds(i * band, band), pl.ds(i * band, extent - i * band)
        swaps.append(
            pltpu.make_async_remote_copy(
                src_ref=grams.at[1 - side, rows, cols], dst_ref=gram_far.at[rows, cols],
                send_sem=far_send.at[i], recv_sem=far_recv.at[i],
                device_id={"fsdp": mate}, device_id_type=MESH,
            )
        )

    half = per_range // 2
    far_off = n_dp // 2
    ways = (
        (1, up, sums_up, up_send, up_recv, pl.ds(0, half)),
        (-1, down, sums_down, down_send, down_recv, pl.ds(half, per_range - half)),
    )

    def columns(c):
        return pl.ds(c * width, width)

    def ring_copy(way, c, step):
        sign, target, sums, send, recv, part = way
        dest = lax.rem(dp + sign * (far_off - step) + n_dp, n_dp)
        if step == 0:
            src = grad_v.at[dest, part, :, columns(c)]
            dst = sums.at[0, part, :, columns(c)]
        else:
            src = sums.at[step - 1, :, :, columns(c)]
            dst = sums.at[step, :, :, columns(c)]
        return pltpu.make_async_remote_copy(
            src_ref=src, dst_ref=dst, send_sem=send.at[c, step], recv_sem=recv.at[c, step],
            device_id={"dp": target}, device_id_type=MESH,
        )

    def ring_step(c, step):
        for way in ways:
            sign, target, sums, send, recv, part = way
            if step > 0:
                ring_copy(way, c, step - 1).wait_recv()
                dest = lax.rem(dp + sign * (far_off - step) + n_dp, n_dp)
                if step == 1:
                    other = pl.ds(half, per_range - half) if sign == 1 else pl.ds(0, half)
                    sums[0, part, :, columns(c)] = (
                        sums[0, part, :, columns(c)].astype(F32)
                        + grad_v[dest, part, :, columns(c)].astype(F32)
                    ).astype(BF16)
                    sums[0, other, :, columns(c)] = grad_v[dest, other, :, columns(c)]
                else:
                    sums[step - 1, :, :, columns(c)] = (
                        sums[step - 1, :, :, columns(c)].astype(F32)
                        + grad_v[dest, :, :, columns(c)].astype(F32)
                    ).astype(BF16)
            ring_copy(way, c, step).start()

    def finish(c):
        for way in ways:
            ring_copy(way, c, far_off - 1).wait_recv()
        total = (
            grad_v[dp, :, :, columns(c)].astype(F32)
            + sums_up[far_off - 1, :, :, columns(c)].astype(F32)
            + sums_down[far_off - 1, :, :, columns(c)].astype(F32)
        )
        summed[c] = total.astype(BF16)

        def pick(p, carry):
            outgoing[c, p] = summed[c, table[p, 2]]
            return carry

        lax.fori_loop(0, half_count, pick, 0)

        def post(k, carry):
            target = me ^ (n_fsdp - k)
            pltpu.make_async_remote_copy(
                src_ref=outgoing.at[c, lax.rem(target, half_count)],
                dst_ref=stripes.at[me, :, columns(c)],
                send_sem=first_send, recv_sem=first_recv.at[c],
                device_id={"fsdp": target}, device_id_type=MESH,
            ).start()
            return carry

        lax.fori_loop(1, n_fsdp, post, 0)
        stripes[me, :, columns(c)] = outgoing[c, lax.rem(me, half_count)]

    loads[0].wait()
    for c in range(N_CHUNK):
        ring_step(c, 0)
    to_scalars.wait()
    for swap in swaps:
        swap.start()
    order = sorted(
        (0.5 * c + step, -step, c, step) for c in range(N_CHUNK) for step in range(1, far_off + 1)
    )
    for _, _, c, step in order:
        if step < far_off:
            ring_step(c, step)
        else:
            finish(c)

    loads[1].wait()
    loads[2].wait()
    for swap in swaps:
        swap.wait_recv()
    owns = table[0, 3] > 0
    basis = jnp.where(owns, vec_own[...], vec_far[...]).T
    for i in range(n_band):
        for j in range(i, n_band):
            rows, cols = pl.ds(i * band, band), pl.ds(j * band, band)
            tile = jnp.where(owns, gram_own[rows, cols], gram_far[rows, cols])
            gram_own[rows, cols] = tile
            if j > i:
                gram_own[cols, rows] = tile.T
    for c in range(N_CHUNK):
        wait_bytes(stripes.at[pl.ds(0, n_fsdp - 1), :, columns(c)], first_recv.at[c])
    block = stripes[...].astype(F32).reshape(extent, extent)

    @pl.when(side == 0)
    def _():
        iterate_m[...] = block.astype(BF16)

    @pl.when(side == 1)
    def _():
        iterate_m[...] = block.T.astype(BF16)

    matrix = iterate_m[...]
    state = ema_decay * gram_own[...].astype(F32) + (1.0 - ema_decay) * dot_nt(matrix, matrix)
    state_high, state_low = split(state)
    turned = dot_nn(basis, state_high) + dot_nn(basis, state_low)
    turned = turned / jnp.sqrt(jnp.sum(turned * turned, axis=1, keepdims=True) + norm_eps)
    row_at = lax.broadcasted_iota(jnp.int32, (extent, extent), 0)
    col_at = lax.broadcasted_iota(jnp.int32, (extent, extent), 1)
    identity = jnp.where(row_at == col_at, 1.0, 0.0)
    for _ in range(ITERS - 1):
        high = turned.astype(BF16)
        gap = (identity - dot_nt(high, high)).astype(BF16)
        turned = turned + 0.5 * dot_nn(gap, high)
    high = turned.astype(BF16)
    gap = (identity - dot_nt(high, high)).astype(BF16)

    half_rows = extent // 2

    def piece(h, i):
        row = h * half_rows + (i // across) * piece_rows
        col = lax.rem(i, across) * piece_cols
        return (
            pl.ds(pl.multiple_of(row, piece_rows), piece_rows),
            pl.ds(pl.multiple_of(col, piece_cols), piece_cols),
        )

    for h in range(2):
        part = slice(h * half_rows, (h + 1) * half_rows)
        last = turned[:, part] + 0.5 * dot_nn(gap, high[:, part])
        iterate_m[pl.ds(h * half_rows, half_rows), :] = last.T.astype(BF16)

        def spread(k, carry):
            target = me ^ (n_fsdp - k)
            pltpu.make_async_remote_copy(
                src_ref=iterate_m.at[piece(h, target)], dst_ref=held[h].at[me],
                send_sem=second_send, recv_sem=second_recv.at[h],
                device_id={"fsdp": target}, device_id_type=MESH,
            ).start()
            return carry

        lax.fori_loop(1, n_fsdp, spread, 0)
        held[h][me] = iterate_m[piece(h, me)]
        held[h][n_fsdp] = jnp.zeros((piece_rows, piece_cols), BF16)

    def select(h, target, place):
        for t in range(AP_CAP):
            place[h, target, t] = held[h][table[target, t]]

    for h in range(2):
        wait_bytes(held[h].at[pl.ds(0, n_fsdp - 1)], second_recv.at[h])

        def deliver(k, carry):
            offset = n_fsdp - k
            target = me ^ offset
            select(h, target, chosen)
            pltpu.make_async_remote_copy(
                src_ref=chosen.at[h, target], dst_ref=landed.at[h, me],
                send_sem=third_send, recv_sem=third_recv.at[h, offset // group],
                device_id={"fsdp": target}, device_id_type=MESH,
            ).start()
            return carry

        lax.fori_loop(1, n_fsdp, deliver, 0)
        for t in range(AP_CAP):
            landed[h, me, t] = held[h][table[me, t]]

    lane = lax.broadcasted_iota(jnp.int32, (piece_rows, piece_cols), 1)

    def quantize(h, m):
        band_at = (me // across) ^ m
        rows = pl.ds(pl.multiple_of(h * half_rows + band_at * piece_rows, piece_rows), piece_rows)
        for t in range(AP_CAP):
            filled = table[me, t] < n_fsdp
            scales = jnp.zeros((piece_rows, 128), F32)
            for q in range(across):
                value = landed[h, across * band_at + q, t].astype(F32)
                size = jnp.abs(value)
                first = jnp.max(jnp.where(lane < QG, size, 0.0), axis=1, keepdims=True)
                last = jnp.max(jnp.where(lane < QG, 0.0, size), axis=1, keepdims=True)
                first = (first + norm_eps).astype(BF16).astype(F32)
                last = (last + norm_eps).astype(BF16).astype(F32)
                code = value / jnp.where(lane < QG, first, last)
                codes_out[t, rows, pl.ds(q * piece_cols, piece_cols)] = code.astype(BF16)
                scales = jnp.where(lane == 2 * q, first, scales)
                scales = jnp.where(lane == 2 * q + 1, last, scales)
            scale_m[t, rows, :] = jnp.where(filled, scales, 0.0)

    for h in range(2):
        for g in reversed(range(n_fsdp // group)):
            count = group - 1 if g == 0 else group
            wait_bytes(landed.at[h, pl.ds(0, count)], third_recv.at[h, g])

            def several(m, carry):
                quantize(h, m)
                return carry

            lax.fori_loop(g * group // across, (g + 1) * group // across, several, 0)
    n_group = extent // QG
    for t in range(AP_CAP):
        scales_out[t] = scale_m[t].T[:n_group].astype(BF16)

    for swap in swaps:
        swap.wait_send()
    for c in range(N_CHUNK):
        for step in range(far_off):
            for way in ways:
                ring_copy(way, c, step).wait_send()
    for c in range(N_CHUNK):
        wait_bytes(stripes.at[pl.ds(0, n_fsdp - 1), :, columns(c)], first_send)
    for h in range(2):
        wait_bytes(held[h].at[pl.ds(0, n_fsdp - 1)], second_send)
        wait_bytes(landed.at[h, pl.ds(0, n_fsdp - 1)], third_send)


def fill_table(dp, me, half_count, per_range, owner_v, apply_v, table_v):
    n_fsdp = 2 * half_count
    shape = (n_fsdp, owner_v.shape[1])
    ids = lax.broadcasted_iota(jnp.int32, shape, 1) - dp * per_range
    ranks = lax.broadcasted_iota(jnp.int32, shape, 0)
    ours = (ids >= 0) & (ids < per_range)
    owners = jnp.broadcast_to(owner_v[...], shape)
    pairs = owners & (half_count - 1)
    none = 2 * per_range * n_fsdp
    first = jnp.full((n_fsdp, 1), none, jnp.int32)
    last = jnp.full((n_fsdp, 1), -1, jnp.int32)
    for s in range(2):
        hit = ours & (jnp.broadcast_to(apply_v[pl.ds(s, 1), :], shape) == ranks)
        key = (2 * ids + s) * n_fsdp + s * half_count + pairs
        first = jnp.minimum(first, jnp.min(jnp.where(hit, key, none), axis=1, keepdims=True))
        last = jnp.maximum(last, jnp.max(jnp.where(hit, key, -1), axis=1, keepdims=True))
    slot_0 = jnp.where(first < none, first & (n_fsdp - 1), n_fsdp)
    slot_1 = jnp.where(last > first, last & (n_fsdp - 1), n_fsdp)
    block = jnp.max(jnp.where(ours & (pairs == ranks), ids, 0), axis=1, keepdims=True)
    owns = jnp.max(jnp.where(ours & (owners == me), 1, 0), axis=1, keepdims=True)
    lane = lax.broadcasted_iota(jnp.int32, table_v.shape, 1)
    out = jnp.where(lane == 0, slot_0, slot_1)
    out = jnp.where(lane == 2, block, out)
    table_v[...] = jnp.where(lane == 3, owns, out)


def local(grad_parts, owner_map, apply_map, gram_old, old_vectors):
    n_dp = lax.axis_size("dp")
    n_fsdp = lax.axis_size("fsdp")
    per_range = owner_map.shape[0] // n_dp
    stripe, extent = grad_parts.shape[2], grad_parts.shape[3]
    grads = grad_parts.reshape(n_dp, per_range, stripe, extent)
    far_off = n_dp // 2
    width = extent // N_CHUNK
    piece = (extent * 2 // n_fsdp, extent // 4)
    vmem, dma = pltpu.VMEM, pltpu.SemaphoreType.DMA
    in_hbm = [
        pltpu.with_memory_space_constraint(value, pltpu.HBM)
        for value in (owner_map[None], apply_map.T, grads, gram_old[0, 0], old_vectors[0, 0])
    ]
    codes, scales = pl.pallas_call(
        functools.partial(kernel, n_dp, n_fsdp, per_range),
        out_shape=(
            jax.ShapeDtypeStruct((AP_CAP, extent, extent), BF16),
            jax.ShapeDtypeStruct((AP_CAP, extent // QG, extent), BF16),
        ),
        in_specs=[pl.BlockSpec(memory_space=pl.ANY)] * 5,
        out_specs=(pl.BlockSpec(memory_space=pltpu.VMEM), pl.BlockSpec(memory_space=pltpu.VMEM)),
        scratch_shapes=[
            vmem((1, owner_map.shape[0]), jnp.int32),
            vmem((2, owner_map.shape[0]), jnp.int32),
            vmem((n_fsdp, 128), jnp.int32),
            pltpu.SMEM((n_fsdp, 128), jnp.int32),
            vmem((n_dp, per_range, stripe, extent), BF16),
            vmem((far_off, per_range, stripe, extent), BF16),
            vmem((far_off, per_range, stripe, extent), BF16),
            vmem((N_CHUNK, per_range, stripe, width), BF16),
            vmem((N_CHUNK, n_fsdp // 2, stripe, width), BF16),
            vmem((n_fsdp, stripe, extent), BF16),
            vmem((extent, extent), BF16),
            vmem((extent, extent), BF16),
            vmem((extent, extent), BF16),
            vmem((extent, extent), BF16),
            vmem((extent, extent), BF16),
            vmem((n_fsdp + 1,) + piece, BF16),
            vmem((n_fsdp + 1,) + piece, BF16),
            vmem((2, n_fsdp, AP_CAP) + piece, BF16),
            vmem((2, n_fsdp, AP_CAP) + piece, BF16),
            vmem((AP_CAP, extent, 128), F32),
            dma((6,)),
            dma((5,)), dma((5,)),
            dma((N_CHUNK, far_off)), dma((N_CHUNK, far_off)),
            dma((N_CHUNK, far_off)), dma((N_CHUNK, far_off)),
            dma, dma((N_CHUNK,)),
            dma, dma((2,)),
            dma, dma((2, n_fsdp // 8)),
        ],
        compiler_params=pltpu.CompilerParams(
            collective_id=0, has_side_effects=True, vmem_limit_bytes=48 * 2**20
        ),
        name="refresh",
    )(*in_hbm)
    return codes[None, None], jnp.swapaxes(scales, 1, 2)[None, None]


def solution(mesh):
    placed = (
        P("dp", None, "fsdp", None),
        P(),
        P(),
        P("dp", "fsdp", None, None, None),
        P("dp", "fsdp", None, None, None),
    )
    return jax.shard_map(
        local,
        mesh=mesh,
        in_specs=placed,
        out_specs=(P("dp", "fsdp", None, None, None), P("dp", "fsdp", None, None, None)),
        check_vma=False,
    )
```

```python
import functools

import jax
import jax.numpy as jnp
from jax import lax
from jax.experimental import pallas as pl
from jax.experimental.pallas import tpu as pltpu
from jax.sharding import PartitionSpec as P

QG = 64
ITERS = 2
AP_CAP = 2
MESH = pl.DeviceIdType.MESH

ema_decay = 0.95
norm_eps = 1e-06

N_CHUNK = 4
N_STORE = 8
F32 = jnp.float32
BF16 = jnp.bfloat16


def dot_nn(a, b):
    return jnp.dot(a, b, preferred_element_type=F32)


def dot_nt(a, b):
    return lax.dot_general(a, b, (((1,), (1,)), ((), ())), preferred_element_type=F32)


def split(value):
    high = value.astype(BF16)
    return high, (value - high.astype(F32)).astype(BF16)


def wait_bytes(ref, sem):
    pltpu.make_async_copy(ref, ref, sem).wait()


def kernel(
    n_dp, n_fsdp, per_range,
    owner_map, apply_map, grads, grams, vectors,
    codes_out, scales_out,
    owner_v, apply_v, table_v, table,
    grad_v, sums_up, sums_down, summed, outgoing, stripes,
    gram_own, vec_own, gram_far, vec_far, iterate_m, held_upper, held_lower, chosen, landed, scale_m,
    load_sem, far_send, far_recv, up_send, up_recv, down_send, down_recv,
    first_send, first_recv, second_send, second_recv, third_send, third_recv,
):
    dp = lax.axis_index("dp")
    me = lax.axis_index("fsdp")
    half_count = n_fsdp // 2
    side = me // half_count
    extent = gram_own.shape[0]
    width = extent // N_CHUNK
    held = (held_upper, held_lower)
    piece_rows, piece_cols = held_upper.shape[1:]
    across = extent // piece_cols
    group = 8

    loads = [
        pltpu.make_async_copy(grads, grad_v, load_sem.at[0]),
        pltpu.make_async_copy(grams.at[side], gram_own, load_sem.at[1]),
        pltpu.make_async_copy(vectors.at[side], vec_own, load_sem.at[2]),
        pltpu.make_async_copy(owner_map, owner_v, load_sem.at[3]),
        pltpu.make_async_copy(apply_map, apply_v, load_sem.at[4]),
    ]
    for load in loads:
        load.start()

    barrier = pltpu.get_barrier_semaphore()

    def greet(k, carry):
        pl.semaphore_signal(barrier, inc=1, device_id={"fsdp": me ^ k}, device_id_type=MESH)
        return carry

    up = lax.rem(dp + 1, n_dp)
    down = lax.rem(dp + n_dp - 1, n_dp)
    pl.semaphore_signal(barrier, inc=1, device_id={"dp": up}, device_id_type=MESH)
    pl.semaphore_signal(barrier, inc=1, device_id={"dp": down}, device_id_type=MESH)
    lax.fori_loop(1, n_fsdp, greet, 0)
    loads[3].wait()
    loads[4].wait()
    fill_table(dp, me, half_count, per_range, owner_v, apply_v, table_v)
    to_scalars = pltpu.make_async_copy(table_v, table, load_sem.at[5])
    to_scalars.start()
    pl.semaphore_wait(barrier, n_fsdp + 1)

    mate = lax.rem(me + half_count, n_fsdp)
    n_band = 4
    band = extent // n_band
    swaps = [
        pltpu.make_async_remote_copy(
            src_ref=vectors.at[1 - side], dst_ref=vec_far,
            send_sem=far_send.at[n_band], recv_sem=far_recv.at[n_band],
            device_id={"fsdp": mate}, device_id_type=MESH,
        )
    ]
    for i in range(n_band):
        rows, cols = pl.ds(i * band, band), pl.ds(i * band, extent - i * band)
        swaps.append(
            pltpu.make_async_remote_copy(
                src_ref=grams.at[1 - side, rows, cols], dst_ref=gram_far.at[rows, cols],
                send_sem=far_send.at[i], recv_sem=far_recv.at[i],
                device_id={"fsdp": mate}, device_id_type=MESH,
            )
        )

    half = per_range // 2
    far_off = n_dp // 2
    ways = (
        (1, up, sums_up, up_send, up_recv, pl.ds(0, half)),
        (-1, down, sums_down, down_send, down_recv, pl.ds(half, per_range - half)),
    )

    def columns(c):
        return pl.ds(c * width, width)

    def ring_copy(way, c, step):
        sign, target, sums, send, recv, part = way
        dest = lax.rem(dp + sign * (far_off - step) + n_dp, n_dp)
        if step == 0:
            src = grad_v.at[dest, part, :, columns(c)]
            dst = sums.at[0, part, :, columns(c)]
        else:
            src = sums.at[step - 1, :, :, columns(c)]
            dst = sums.at[step, :, :, columns(c)]
        return pltpu.make_async_remote_copy(
            src_ref=src, dst_ref=dst, send_sem=send.at[c, step], recv_sem=recv.at[c, step],
            device_id={"dp": target}, device_id_type=MESH,
        )

    def ring_step(c, step):
        for way in ways:
            sign, target, sums, send, recv, part = way
            if step > 0:
                ring_copy(way, c, step - 1).wait_recv()
                dest = lax.rem(dp + sign * (far_off - step) + n_dp, n_dp)
                if step == 1:
                    other = pl.ds(half, per_range - half) if sign == 1 else pl.ds(0, half)
                    sums[0, part, :, columns(c)] = (
                        sums[0, part, :, columns(c)].astype(F32)
                        + grad_v[dest, part, :, columns(c)].astype(F32)
                    ).astype(BF16)
                    sums[0, other, :, columns(c)] = grad_v[dest, other, :, columns(c)]
                else:
                    sums[step - 1, :, :, columns(c)] = (
                        sums[step - 1, :, :, columns(c)].astype(F32)
                        + grad_v[dest, :, :, columns(c)].astype(F32)
                    ).astype(BF16)
            ring_copy(way, c, step).start()

    def finish(c):
        for way in ways:
            ring_copy(way, c, far_off - 1).wait_recv()
        total = (
            grad_v[dp, :, :, columns(c)].astype(F32)
            + sums_up[far_off - 1, :, :, columns(c)].astype(F32)
            + sums_down[far_off - 1, :, :, columns(c)].astype(F32)
        )
        summed[c] = total.astype(BF16)

        def pick(p, carry):
            outgoing[c, p] = summed[c, table[p, 2]]
            return carry

        lax.fori_loop(0, half_count, pick, 0)

        def post(k, carry):
            target = me ^ (n_fsdp - k)
            pltpu.make_async_remote_copy(
                src_ref=outgoing.at[c, lax.rem(target, half_count)],
                dst_ref=stripes.at[me, :, columns(c)],
                send_sem=first_send, recv_sem=first_recv.at[c],
                device_id={"fsdp": target}, device_id_type=MESH,
            ).start()
            return carry

        lax.fori_loop(1, n_fsdp, post, 0)
        stripes[me, :, columns(c)] = outgoing[c, lax.rem(me, half_count)]

    loads[0].wait()
    for c in range(N_CHUNK):
        ring_step(c, 0)
    to_scalars.wait()
    for swap in swaps:
        swap.start()
    order = sorted(
        (0.5 * c + step, -step, c, step) for c in range(N_CHUNK) for step in range(1, far_off + 1)
    )
    for _, _, c, step in order:
        if step < far_off:
            ring_step(c, step)
        else:
            finish(c)

    loads[1].wait()
    loads[2].wait()
    for swap in swaps:
        swap.wait_recv()
    owns = table[0, 3] > 0
    basis = jnp.where(owns, vec_own[...], vec_far[...]).T
    for i in range(n_band):
        for j in range(i, n_band):
            rows, cols = pl.ds(i * band, band), pl.ds(j * band, band)
            tile = jnp.where(owns, gram_own[rows, cols], gram_far[rows, cols])
            gram_own[rows, cols] = tile
            if j > i:
                gram_own[cols, rows] = tile.T
    for c in range(N_CHUNK):
        wait_bytes(stripes.at[pl.ds(0, n_fsdp - 1), :, columns(c)], first_recv.at[c])
    block = stripes[...].astype(F32).reshape(extent, extent)

    @pl.when(side == 0)
    def _():
        iterate_m[...] = block.astype(BF16)

    @pl.when(side == 1)
    def _():
        iterate_m[...] = block.T.astype(BF16)

    matrix = iterate_m[...]
    state = ema_decay * gram_own[...].astype(F32) + (1.0 - ema_decay) * dot_nt(matrix, matrix)
    state_high, state_low = split(state)
    turned = dot_nn(basis, state_high) + dot_nn(basis, state_low)
    turned = turned / jnp.sqrt(jnp.sum(turned * turned, axis=1, keepdims=True) + norm_eps)
    row_at = lax.broadcasted_iota(jnp.int32, (extent, extent), 0)
    col_at = lax.broadcasted_iota(jnp.int32, (extent, extent), 1)
    identity = jnp.where(row_at == col_at, 1.0, 0.0)
    for _ in range(ITERS - 1):
        high, low = split(turned)
        cross = dot_nt(high, low)
        gap = ((identity - dot_nt(high, high)) - (cross + cross.T)).astype(BF16)
        turned = turned + 0.5 * dot_nn(gap, high)
    high = turned.astype(BF16)
    gap = (identity - dot_nt(high, high)).astype(BF16)

    half_rows = extent // 2

    def piece(h, i):
        row = h * half_rows + (i // across) * piece_rows
        col = lax.rem(i, across) * piece_cols
        return (
            pl.ds(pl.multiple_of(row, piece_rows), piece_rows),
            pl.ds(pl.multiple_of(col, piece_cols), piece_cols),
        )

    for h in range(2):
        part = slice(h * half_rows, (h + 1) * half_rows)
        last = turned[:, part] + 0.5 * dot_nn(gap, high[:, part])
        iterate_m[pl.ds(h * half_rows, half_rows), :] = last.T.astype(BF16)

        def spread(k, carry):
            target = me ^ (n_fsdp - k)
            pltpu.make_async_remote_copy(
                src_ref=iterate_m.at[piece(h, target)], dst_ref=held[h].at[me],
                send_sem=second_send, recv_sem=second_recv.at[h],
                device_id={"fsdp": target}, device_id_type=MESH,
            ).start()
            return carry

        lax.fori_loop(1, n_fsdp, spread, 0)
        held[h][me] = iterate_m[piece(h, me)]
        held[h][n_fsdp] = jnp.zeros((piece_rows, piece_cols), BF16)

    def select(h, target, place):
        for t in range(AP_CAP):
            place[h, target, t] = held[h][table[target, t]]

    for h in range(2):
        wait_bytes(held[h].at[pl.ds(0, n_fsdp - 1)], second_recv.at[h])

        def deliver(k, carry):
            offset = n_fsdp - k
            target = me ^ offset
            select(h, target, chosen)
            pltpu.make_async_remote_copy(
                src_ref=chosen.at[h, target], dst_ref=landed.at[h, me],
                send_sem=third_send, recv_sem=third_recv.at[h, offset // group],
                device_id={"fsdp": target}, device_id_type=MESH,
            ).start()
            return carry

        lax.fori_loop(1, n_fsdp, deliver, 0)
        for t in range(AP_CAP):
            landed[h, me, t] = held[h][table[me, t]]

    lane = lax.broadcasted_iota(jnp.int32, (piece_rows, piece_cols), 1)

    def quantize(h, m):
        band_at = (me // across) ^ m
        rows = pl.ds(pl.multiple_of(h * half_rows + band_at * piece_rows, piece_rows), piece_rows)
        for t in range(AP_CAP):
            filled = table[me, t] < n_fsdp
            scales = jnp.zeros((piece_rows, 128), F32)
            for q in range(across):
                value = landed[h, across * band_at + q, t].astype(F32)
                size = jnp.abs(value)
                first = jnp.max(jnp.where(lane < QG, size, 0.0), axis=1, keepdims=True)
                last = jnp.max(jnp.where(lane < QG, 0.0, size), axis=1, keepdims=True)
                first = (first + norm_eps).astype(BF16).astype(F32)
                last = (last + norm_eps).astype(BF16).astype(F32)
                code = value / jnp.where(lane < QG, first, last)
                codes_out[t, rows, pl.ds(q * piece_cols, piece_cols)] = code.astype(BF16)
                scales = jnp.where(lane == 2 * q, first, scales)
                scales = jnp.where(lane == 2 * q + 1, last, scales)
            scale_m[t, rows, :] = jnp.where(filled, scales, 0.0)

    for h in range(2):
        for g in reversed(range(n_fsdp // group)):
            count = group - 1 if g == 0 else group
            wait_bytes(landed.at[h, pl.ds(0, count)], third_recv.at[h, g])

            def several(m, carry):
                quantize(h, m)
                return carry

            lax.fori_loop(g * group // across, (g + 1) * group // across, several, 0)
    n_group = extent // QG
    for t in range(AP_CAP):
        scales_out[t] = scale_m[t].T[:n_group].astype(BF16)

    for swap in swaps:
        swap.wait_send()
    for c in range(N_CHUNK):
        for step in range(far_off):
            for way in ways:
                ring_copy(way, c, step).wait_send()
    for c in range(N_CHUNK):
        wait_bytes(stripes.at[pl.ds(0, n_fsdp - 1), :, columns(c)], first_send)
    for h in range(2):
        wait_bytes(held[h].at[pl.ds(0, n_fsdp - 1)], second_send)
        wait_bytes(landed.at[h, pl.ds(0, n_fsdp - 1)], third_send)


def fill_table(dp, me, half_count, per_range, owner_v, apply_v, table_v):
    n_fsdp = 2 * half_count
    shape = (n_fsdp, owner_v.shape[1])
    ids = lax.broadcasted_iota(jnp.int32, shape, 1) - dp * per_range
    ranks = lax.broadcasted_iota(jnp.int32, shape, 0)
    ours = (ids >= 0) & (ids < per_range)
    owners = jnp.broadcast_to(owner_v[...], shape)
    pairs = owners & (half_count - 1)
    none = 2 * per_range * n_fsdp
    first = jnp.full((n_fsdp, 1), none, jnp.int32)
    last = jnp.full((n_fsdp, 1), -1, jnp.int32)
    for s in range(2):
        hit = ours & (jnp.broadcast_to(apply_v[pl.ds(s, 1), :], shape) == ranks)
        key = (2 * ids + s) * n_fsdp + s * half_count + pairs
        first = jnp.minimum(first, jnp.min(jnp.where(hit, key, none), axis=1, keepdims=True))
        last = jnp.maximum(last, jnp.max(jnp.where(hit, key, -1), axis=1, keepdims=True))
    slot_0 = jnp.where(first < none, first & (n_fsdp - 1), n_fsdp)
    slot_1 = jnp.where(last > first, last & (n_fsdp - 1), n_fsdp)
    block = jnp.max(jnp.where(ours & (pairs == ranks), ids, 0), axis=1, keepdims=True)
    owns = jnp.max(jnp.where(ours & (owners == me), 1, 0), axis=1, keepdims=True)
    lane = lax.broadcasted_iota(jnp.int32, table_v.shape, 1)
    out = jnp.where(lane == 0, slot_0, slot_1)
    out = jnp.where(lane == 2, block, out)
    table_v[...] = jnp.where(lane == 3, owns, out)


def store(codes, scales, codes_out, scales_out, sems):
    rows = AP_CAP * codes.shape[1] // N_STORE
    per_slot = codes.shape[1] // rows
    copies = [pltpu.make_async_copy(scales, scales_out, sems.at[N_STORE])]
    for i in range(N_STORE):
        at = (i // per_slot, pl.ds(i % per_slot * rows, rows))
        copies.append(pltpu.make_async_copy(codes.at[at], codes_out.at[at], sems.at[i]))
    for copy in copies:
        copy.start()
    for copy in copies:
        copy.wait()


def local(grad_parts, owner_map, apply_map, gram_old, old_vectors):
    n_dp = lax.axis_size("dp")
    n_fsdp = lax.axis_size("fsdp")
    per_range = owner_map.shape[0] // n_dp
    stripe, extent = grad_parts.shape[2], grad_parts.shape[3]
    grads = grad_parts.reshape(n_dp, per_range, stripe, extent)
    far_off = n_dp // 2
    width = extent // N_CHUNK
    piece = (extent * 2 // n_fsdp, extent // 4)
    vmem, dma = pltpu.VMEM, pltpu.SemaphoreType.DMA
    in_hbm = [
        pltpu.with_memory_space_constraint(value, pltpu.HBM)
        for value in (owner_map[None], apply_map.T, grads, gram_old[0, 0], old_vectors[0, 0])
    ]
    codes, scales = pl.pallas_call(
        functools.partial(kernel, n_dp, n_fsdp, per_range),
        out_shape=(
            jax.ShapeDtypeStruct((AP_CAP, extent, extent), BF16),
            jax.ShapeDtypeStruct((AP_CAP, extent // QG, extent), BF16),
        ),
        in_specs=[pl.BlockSpec(memory_space=pl.ANY)] * 5,
        out_specs=(pl.BlockSpec(memory_space=pltpu.VMEM), pl.BlockSpec(memory_space=pltpu.VMEM)),
        scratch_shapes=[
            vmem((1, owner_map.shape[0]), jnp.int32),
            vmem((2, owner_map.shape[0]), jnp.int32),
            vmem((n_fsdp, 128), jnp.int32),
            pltpu.SMEM((n_fsdp, 128), jnp.int32),
            vmem((n_dp, per_range, stripe, extent), BF16),
            vmem((far_off, per_range, stripe, extent), BF16),
            vmem((far_off, per_range, stripe, extent), BF16),
            vmem((N_CHUNK, per_range, stripe, width), BF16),
            vmem((N_CHUNK, n_fsdp // 2, stripe, width), BF16),
            vmem((n_fsdp, stripe, extent), BF16),
            vmem((extent, extent), BF16),
            vmem((extent, extent), BF16),
            vmem((extent, extent), BF16),
            vmem((extent, extent), BF16),
            vmem((extent, extent), BF16),
            vmem((n_fsdp + 1,) + piece, BF16),
            vmem((n_fsdp + 1,) + piece, BF16),
            vmem((2, n_fsdp, AP_CAP) + piece, BF16),
            vmem((2, n_fsdp, AP_CAP) + piece, BF16),
            vmem((AP_CAP, extent, 128), F32),
            dma((6,)),
            dma((5,)), dma((5,)),
            dma((N_CHUNK, far_off)), dma((N_CHUNK, far_off)),
            dma((N_CHUNK, far_off)), dma((N_CHUNK, far_off)),
            dma, dma((N_CHUNK,)),
            dma, dma((2,)),
            dma, dma((2, n_fsdp // 8)),
        ],
        compiler_params=pltpu.CompilerParams(
            collective_id=0, has_side_effects=True, vmem_limit_bytes=48 * 2**20
        ),
        name="refresh",
    )(*in_hbm)
    codes, scales = pl.pallas_call(
        store,
        out_shape=(
            jax.ShapeDtypeStruct(codes.shape, BF16), jax.ShapeDtypeStruct(scales.shape, BF16)
        ),
        in_specs=[pl.BlockSpec(memory_space=pltpu.VMEM)] * 2,
        out_specs=[pl.BlockSpec(memory_space=pl.ANY)] * 2,
        scratch_shapes=[dma((N_STORE + 1,))],
        compiler_params=pltpu.CompilerParams(vmem_limit_bytes=8 * 2**20),
        name="store",
    )(codes, scales)
    return codes[None, None], jnp.swapaxes(scales, 1, 2)[None, None]


def solution(mesh):
    placed = (
        P("dp", None, "fsdp", None),
        P(),
        P(),
        P("dp", "fsdp", None, None, None),
        P("dp", "fsdp", None, None, None),
    )
    return jax.shard_map(
        local,
        mesh=mesh,
        in_specs=placed,
        out_specs=(P("dp", "fsdp", None, None, None), P("dp", "fsdp", None, None, None)),
        check_vma=False,
    )
```
